32 devices in a mesh: parts: 2 (over x), step: 16 (over z, y, core).
Axes of the slice: x: 2, y: 2, z: 4, core: 2. Of those that a mesh axis runs over, the one named last changes fastest.
Arguments:
- propagators: float32 [32, 1024, 1024], P(('parts', 'step')), parts along dimension 0, may hold values from -1 to 1
- forcing: float32 [32, 1024], P(('parts', 'step')), parts along dimension 0, may hold values from -3 to 3
- starts: float32 [32, 256], P(('parts', 'step')), parts along dimension 0, may hold values from -6 to 6
- directions: float32 [32, 64, 1024], P(('parts', 'step')), parts along dimension 0, may hold values from -6 to 6
Outputs:
- residual: float32 [32, 256], P(('parts', 'step')), parts along dimension 0
- jacobian_rows: float32 [32, 64, 1024], P(('parts', 'step')), parts along dimension 0
The draws below stay inside these ranges and needn't reach their ends.
There are 2 independent parts, one for each index of `parts`. The reference program is written for one: setup_inputs(seed, part) draws one part's arguments, and reference() takes and returns one part's arrays. A program takes and returns all parts, laid end to end along the dimension named above; each array names one. Nothing has to cross between parts.
All inputs are finite; a program needn't handle non-finite values.
Results may differ from the reference program's by a relative error of at most 0.00012.
Values sent between devices are 32-bit elements; how exact they have to be, the bound alone decides.
No kernel may reach another device: no remote copies, remote signals or barrier semaphores. Data moves between devices by JAX's collectives and lax.ppermute only.
A program may use at most 64 MiB of HBM per device.

```python
import math
import jax
import jax.numpy as jnp
from jax import lax

N = 1024
WIN = 4
ROWS_DEV = 64
STEPS = 16


def draw_propagators(key, part):
    key = jax.random.fold_in(key, 11)
    key_diag, key_off = jax.random.split(key)
    diag_vals = jax.random.uniform(key_diag, (STEPS, N), jnp.float32, 0.6, 1.0)
    off_vals = jax.random.normal(key_off, (STEPS, N, N), jnp.float32) * (0.3 / math.sqrt(N))
    off_vals = jnp.clip(off_vals, -0.9, 0.9)
    rows_idx = lax_iota(N)
    identity = (rows_idx[:, None] == rows_idx[None, :]).astype(jnp.float32)
    return off_vals * (1.0 - identity) + identity * diag_vals[:, :, None]


def lax_iota(count):
    return jnp.arange(count, dtype=jnp.int32)


def block_scale(own_key, extent, shards, low, top_value):
    level = 1.0
    for dim, parts in shards:
        heights = jax.random.uniform(jax.random.fold_in(jax.random.fold_in(own_key, 6), dim), (parts,), jnp.float32, low / len(shards), top_value / len(shards))
        level = level * jnp.repeat(jnp.exp(heights), extent[dim] // parts).reshape((-1,) + (1,) * (len(extent) - 1 - dim))
    return level


def noise(rng, dims, scale, most, cuts=(), kind=jnp.bfloat16):
    result = jax.random.normal(rng, dims, jnp.float32) * scale
    if len(cuts) > 0:
        result = block_scale(rng, dims, cuts, -0.22, 0.18) * result
    return jnp.clip(result, min=-most, max=most).astype(kind)


def setup_inputs(seed: int = 0, part: int = 0) -> dict:
    streams_of = jax.random.split(jax.random.key(seed), 5)
    part_keys = jax.random.split(jax.random.fold_in(streams_of[4], part), 5)
    propagators = draw_propagators(jax.random.fold_in(jax.random.fold_in(streams_of[4], part), 71), part)
    forcing = noise(part_keys[1], (STEPS, N), 0.5, 3.0, ((0, 16),), jnp.float32)
    starts = noise(part_keys[2], (STEPS, N // WIN), 1.0, 6.0, ((0, 16),), jnp.float32)
    directions = noise(part_keys[3], (STEPS, ROWS_DEV, N), 1.0, 6.0, ((0, 16),), jnp.float32)
    return {"propagators": propagators, "forcing": forcing, "starts": starts, "directions": directions}


def reference(propagators, forcing, starts, directions):
    count = STEPS // WIN
    mats = propagators.reshape(count, WIN, N, N)
    sources = forcing.reshape(count, WIN, N)
    states = starts.reshape(count, N)
    images = directions.reshape(count, WIN * ROWS_DEV, N)
    for position in range(WIN):
        step_mat = mats[:, position]
        states = jnp.einsum("wij,wj->wi", step_mat, states, precision=lax.Precision.HIGHEST) + sources[:, position]
        images = jnp.einsum("wkj,wij->wki", images, step_mat, precision=lax.Precision.HIGHEST)
    residual = jnp.roll(states, 1, axis=0) - starts.reshape(count, N)
    jacobian_rows = jnp.roll(images, 1, axis=0) - directions.reshape(count, WIN * ROWS_DEV, N)
    return residual.reshape(STEPS, N // WIN), jacobian_rows.reshape(STEPS, ROWS_DEV, N)
```

```python
import functools

import jax
import jax.numpy as jnp
from jax import lax
from jax.experimental import pallas as pl
from jax.experimental.pallas import tpu as pltpu
from jax.sharding import PartitionSpec as P

WIN = 4
VMEM = pl.BlockSpec(memory_space=pltpu.VMEM)
PAD = 8


def swapped(block, bit):
    count = lax.axis_size("step")
    return lax.ppermute(block, "step", [(i, i ^ bit) for i in range(count)])


def product_nt(left, right):
    return lax.dot_general(left, right, (((1,), (1,)), ((), ())), preferred_element_type=jnp.float32)


def high_low(value):
    high = value.astype(jnp.bfloat16)
    return high, (value - high.astype(jnp.float32)).astype(jnp.bfloat16)


def times(x, high, low):
    rows = x.shape[0]
    x_high = x.astype(jnp.bfloat16).astype(jnp.float32)
    both = jnp.concatenate([x_high, x - x_high], 0).astype(jnp.bfloat16)
    wide = product_nt(both, high)
    narrow = product_nt(both[: (rows + 15) // 16 * 16], low)
    return wide[:rows] + wide[rows:] + narrow[:rows]


def two_steps(x, maps, sources, state):
    for k in range(2):
        x = times(x, maps[0, k], maps[1, k])
        if state:
            row = lax.broadcasted_iota(jnp.int32, (PAD, x.shape[1]), 0)
            tail = x[-PAD:] + jnp.where(row == 0, sources[k], 0.0)
            x = jnp.concatenate([x[:-PAD], tail], 0)
    return x


def load_sources(own_f, other_f, core):
    own, other = own_f[...], other_f[...]
    return jnp.where(core == 0, own, other), jnp.where(core == 0, other, own)


def first_kernel(rows_ref, own_s, s1, s2, s3, own_f, other_f, own_p, other_p, out, maps):
    place = lax.axis_index("step") % WIN
    core = place % 2
    maps[0, core], maps[1, core] = high_low(own_p[...])
    maps[0, 1 - core], maps[1, 1 - core] = high_low(other_p[...])
    slices = (own_s[...], s1[...], s2[...], s3[...])
    ordered = []
    for j in range(WIN):
        flip = j ^ place
        pick = slices[0]
        for k in range(1, WIN):
            pick = jnp.where(flip == k, slices[k], pick)
        ordered.append(pick)
    x0 = jnp.concatenate(ordered, 1)
    row = lax.broadcasted_iota(jnp.int32, (PAD, x0.shape[1]), 0)
    x = jnp.concatenate([rows_ref[...], jnp.where(row == 0, x0, 0.0)], 0)
    out[...] = two_steps(x, maps, load_sources(own_f, other_f, core), True)


def rows_kernel(rows_ref, maps, out):
    out[...] = two_steps(rows_ref[...], maps, None, False)


def state_kernel(rows_ref, own_f, other_f, maps, out):
    core = lax.axis_index("step") % 2
    out[...] = two_steps(rows_ref[...], maps, load_sources(own_f, other_f, core), True)


def rows_and_state_kernel(rows_ref, state_ref, maps, out):
    count = rows_ref.shape[0]
    out[:count] = two_steps(rows_ref[...], maps, None, False)
    out[count:] = state_ref[count:]


def last_kernel(near, far, starts, directions, residual, jacobian):
    place = lax.axis_index("step") % WIN
    count = directions.shape[0]
    width = starts.shape[1]
    second = place >= WIN // 2
    jacobian[...] = jnp.where(second, near[:count], far[:count]) - directions[...]
    end = jnp.where(second, near[count : count + 1], far[count : count + 1])
    mine = end[:, :width]
    for j in range(1, WIN):
        mine = jnp.where(place == j, end[:, j * width : (j + 1) * width], mine)
    residual[...] = mine - starts[...]


def call(body, out_shape, *args):
    return pl.pallas_call(
        body,
        out_shape=out_shape,
        in_specs=[VMEM] * len(args),
        out_specs=jax.tree.map(lambda _: VMEM, out_shape),
        compiler_params=pltpu.CompilerParams(vmem_limit_bytes=40 << 20),
    )(*args)


def local(propagators, forcing, starts, directions):
    own_p, rows = propagators[0], directions[0]
    order = own_p.shape[0]
    count = rows.shape[0]
    steps = lax.axis_size("step")
    f32 = functools.partial(jax.ShapeDtypeStruct, dtype=jnp.float32)
    other_p = swapped(own_p, 1)
    other_rows = swapped(rows, 2)
    other_f = swapped(forcing, 1)
    s1, s2, s3 = (swapped(starts, k) for k in range(1, WIN))
    x_b, maps = call(
        first_kernel,
        (f32((count + PAD, order)), jax.ShapeDtypeStruct((2, 2, order, order), jnp.bfloat16)),
        other_rows, starts, s1, s2, s3, forcing, other_f, own_p, other_p,
    )
    got_b = swapped(x_b, 2)
    x_a = call(rows_kernel, f32((count, order)), rows, maps)
    got_a = swapped(x_a, 2)
    y_b = call(state_kernel, f32((count + PAD, order)), got_b, forcing, other_f, maps)
    near = lax.ppermute(
        y_b, "step", [(i, (i + WIN) % steps if i % WIN >= WIN // 2 else i ^ 1) for i in range(steps)]
    )
    y_a = call(rows_and_state_kernel, f32((count + PAD, order)), got_a, y_b, maps)
    far = lax.ppermute(
        y_a, "step",
        [(i, (i + WIN - 2) % steps if i % WIN >= WIN // 2 else i + 2) for i in range(steps)],
    )
    residual, jacobian = call(last_kernel, (f32(starts.shape), f32(rows.shape)), near, far, starts, rows)
    return residual, jacobian[None]


def solution(mesh):
    return jax.shard_map(
        local,
        mesh=mesh,
        in_specs=(
            P(("parts", "step"), None, None),
            P(("parts", "step"), None),
            P(("parts", "step"), None),
            P(("parts", "step"), None, None),
        ),
        out_specs=(P(("parts", "step"), None), P(("parts", "step"), None, None)),
        check_vma=False,
    )
```

```python
import functools

import jax
import jax.numpy as jnp
from jax import lax
from jax.experimental import pallas as pl
from jax.experimental.pallas import tpu as pltpu
from jax.sharding import PartitionSpec as P

WIN = 4
HALF = WIN // 2
PAD = 8
PIECES = 4
VMEM = pl.BlockSpec(memory_space=pltpu.VMEM)
ANY = pl.BlockSpec(memory_space=pl.ANY)


def swapped(block, bit):
    count = lax.axis_size("step")
    return lax.ppermute(block, "step", [(i, i ^ bit) for i in range(count)])


def product_nt(left, right):
    return lax.dot_general(left, right, (((1,), (1,)), ((), ())), preferred_element_type=jnp.float32)


def high_low(value):
    high = value.astype(jnp.bfloat16)
    return high, (value - high.astype(jnp.float32)).astype(jnp.bfloat16)


def stacked(x):
    high = x.astype(jnp.bfloat16).astype(jnp.float32)
    return jnp.concatenate([high, x - high], 0).astype(jnp.bfloat16)


def times(both, high, low):
    rows = both.shape[0] // 2
    wide = product_nt(both, high)
    narrow = product_nt(both[: (rows + 15) // 16 * 16], low)
    return wide[:rows] + wide[rows:] + narrow[:rows]


def one_row(at, value):
    row = lax.broadcasted_iota(jnp.int32, (PAD, value.shape[1]), 0)
    return jnp.where(row == at, value, 0.0)


def by_core(body):
    core = lax.axis_index("step") % 2
    for k in range(2):
        pl.when(core == k)(functools.partial(body, k))


def own_kernel(own_p, maps):
    maps[0], maps[1] = high_low(own_p[...])


def first_kernel(mirror_v, own_v, v0, v1, v2, v3, own, other_p, out_b, out_a, other, forces):
    place = lax.axis_index("step") % WIN
    rows = out_a.shape[0]
    order = other_p.shape[0]
    part = order // PIECES

    def split_times(both):
        columns = []
        for k in range(PIECES):
            at = pl.ds(k * part, part)
            high, low = high_low(other_p[at])
            other[0, at] = high
            other[1, at] = low
            columns.append(times(both, high, low))
        return jnp.concatenate(columns, 1)

    vectors = (v0[...], v1[...], v2[...], v3[...])
    width = vectors[0].shape[1] - order
    slices = []
    for j in range(WIN):
        pick = vectors[0][:, :width]
        for flip in range(1, WIN):
            pick = jnp.where(j ^ place == flip, vectors[flip][:, :width], pick)
        slices.append(pick)
    x0 = jnp.concatenate(slices, 1)
    even = place % 2 == 0
    own_f, other_f = vectors[0][:, width:], vectors[1][:, width:]
    forces[0] = one_row(0, jnp.where(even, own_f, other_f))
    forces[1] = one_row(0, jnp.where(even, other_f, own_f))

    def body(k):
        x = jnp.concatenate([mirror_v[...], own_v[...], one_row(0, x0)], 0)
        for step in range(2):
            both = stacked(x)
            y = times(both, own[0], own[1]) if step == k else split_times(both)
            x = jnp.concatenate([y[:-PAD], y[-PAD:] + forces[step]], 0)
        out_b[:rows] = x[:rows]
        out_b[rows:] = x[2 * rows :]
        out_a[...] = x[rows : 2 * rows]

    by_core(body)


def state_kernel(got, forces, own, other, out):
    def body(k):
        maps = (own, other) if k == 0 else (other, own)
        x = got[...]
        for step in range(2):
            y = times(stacked(x), maps[step][0], maps[step][1])
            x = jnp.concatenate([y[:-PAD], y[-PAD:] + forces[step]], 0)
        out[...] = x

    by_core(body)


def rows_kernel(got, with_state, own, other, out):
    def body(k):
        maps = (own, other) if k == 0 else (other, own)
        x = got[...]
        for step in range(2):
            x = times(stacked(x), maps[step][0], maps[step][1])
        out[: x.shape[0]] = x
        out[x.shape[0] :] = with_state[x.shape[0] :]

    by_core(body)


def near_kernel(near, starts, directions, residual, jacobian):
    place = lax.axis_index("step") % WIN
    later = place >= HALF
    rows = directions.shape[0]
    width = starts.shape[1]
    jacobian[...] = jnp.where(later, near[:rows], 0.0) - directions[...]
    mine = slice_of(near[rows : rows + 1], place, width)
    residual[...] = jnp.where(later, mine, 0.0) - starts[...]


def slice_of(end, place, width):
    mine = end[:, :width]
    for j in range(1, WIN):
        mine = jnp.where(place == j, end[:, j * width : (j + 1) * width], mine)
    return mine


def far_kernel(far, near_residual, near_jacobian, residual, jacobian):
    place = lax.axis_index("step") % WIN
    first = place < HALF
    rows = near_jacobian.shape[0]
    jacobian[...] = jnp.where(first, far[:rows], 0.0) + near_jacobian[...]
    mine = slice_of(far[rows : rows + 1], place, residual.shape[1])
    residual[...] = jnp.where(first, mine, 0.0) + near_residual[...]


def call(body, micros, out_shape, *args, specs=None, scratch=(), after=()):
    count, extra = len(args), len(after)

    def run(*refs):
        body(*refs[:count], *refs[count + extra :])

    return pl.pallas_call(
        run,
        out_shape=out_shape,
        in_specs=(specs or [VMEM] * count) + [ANY] * extra,
        out_specs=jax.tree.map(lambda _: VMEM, out_shape),
        scratch_shapes=scratch,
        compiler_params=pltpu.CompilerParams(vmem_limit_bytes=20 << 20),
        cost_estimate=pl.CostEstimate(flops=int(micros * 1e9), bytes_accessed=1, transcendentals=0),
    )(*args, *after)


def local(propagators, forcing, starts, directions):
    own_p, own_v = propagators[0], directions[0]
    order = own_p.shape[0]
    rows = own_v.shape[0]
    steps = lax.axis_size("step")
    f32 = functools.partial(jax.ShapeDtypeStruct, dtype=jnp.float32)
    split = jax.ShapeDtypeStruct((2, order, order), jnp.bfloat16)
    tall = f32((rows + PAD, order))
    other_p = swapped(own_p, 1)
    mirror_v = swapped(own_v, 2)
    vector = jnp.concatenate([starts, forcing], 1)
    vectors = [vector] + [swapped(vector, k) for k in range(1, WIN)]
    own = call(own_kernel, 1, split, own_p)
    x_b, x_a, other, forces = call(
        first_kernel, 3, (tall, f32((rows, order)), split, f32((2, PAD, order))), mirror_v, own_v, *vectors, own, other_p
    )
    got_b = swapped(x_b, 2)
    got_a = swapped(x_a, 2)
    y_b = call(state_kernel, 3, tall, got_b, forces, own, other)
    near = lax.ppermute(
        y_b, "step", [(i, (i + WIN) % steps if i % WIN >= HALF else i ^ 1) for i in range(steps)]
    )
    y_a = call(rows_kernel, 3, tall, got_a, y_b, own, other)
    far = lax.ppermute(
        y_a, "step", [(i, (i + WIN - HALF) % steps if i % WIN >= HALF else i + HALF) for i in range(steps)]
    )
    results = f32(starts.shape), f32(own_v.shape)
    near_results = call(near_kernel, 1, results, near, starts, own_v)
    residual, jacobian = call(far_kernel, 1, results, far, *near_results)
    return residual, jacobian[None]


def solution(mesh):
    return jax.shard_map(
        local,
        mesh=mesh,
        in_specs=(
            P(("parts", "step"), None, None),
            P(("parts", "step"), None),
            P(("parts", "step"), None),
            P(("parts", "step"), None, None),
        ),
        out_specs=(P(("parts", "step"), None), P(("parts", "step"), None, None)),
        check_vma=False,
    )
```

```python
import functools

import jax
import jax.numpy as jnp
from jax import lax
from jax.experimental import pallas as pl
from jax.experimental.pallas import tpu as pltpu
from jax.sharding import PartitionSpec as P

WIN = 4
HALF = WIN // 2
PAD = 8
PIECES = 4
VMEM = pl.BlockSpec(memory_space=pltpu.VMEM)
ANY = pl.BlockSpec(memory_space=pl.ANY)


def swapped(block, bit):
    count = lax.axis_size("step")
    return lax.ppermute(block, "step", [(i, i ^ bit) for i in range(count)])


def product_nt(left, right):
    return lax.dot_general(left, right, (((1,), (1,)), ((), ())), preferred_element_type=jnp.float32)


def high_low(value):
    high = value.astype(jnp.bfloat16)
    return high, (value - high.astype(jnp.float32)).astype(jnp.bfloat16)


def stacked(x):
    high = x.astype(jnp.bfloat16).astype(jnp.float32)
    return jnp.concatenate([high, x - high], 0).astype(jnp.bfloat16)


def times(both, high, low):
    rows = both.shape[0] // 2
    wide = product_nt(both, high)
    narrow = product_nt(both[: (rows + 15) // 16 * 16], low)
    return wide[:rows] + wide[rows:] + narrow[:rows]


def one_row(at, value):
    row = lax.broadcasted_iota(jnp.int32, (PAD, value.shape[1]), 0)
    return jnp.where(row == at, value, 0.0)


def own_kernel(own_p, maps):
    maps[0], maps[1] = high_low(own_p[...])


def whole_start(vectors, width):
    place = lax.axis_index("step") % WIN
    ordered = []
    for j in range(WIN):
        pick = vectors[0][:, :width]
        for flip in range(1, WIN):
            pick = jnp.where(j ^ place == flip, vectors[flip][:, :width], pick)
        ordered.append(pick)
    return jnp.concatenate(ordered, 1)


def on_second_chip():
    return lax.axis_index("step") % WIN >= HALF


def by_place(body):
    place = lax.axis_index("step") % WIN
    for k in range(WIN):
        pl.when(place == k)(functools.partial(body, k // 2, k % 2))


def product_rows(later, earlier_high, earlier_low):
    rows = later.shape[0]
    both = stacked(later)
    dot = functools.partial(jnp.dot, preferred_element_type=jnp.float32)
    wide = dot(both, earlier_high)
    return wide[:rows] + wide[rows:] + dot(both[:rows], earlier_low)


def joint_rows(joint, low, later, earlier):
    order = later.shape[0]
    part = order // PIECES
    for at in range(0, joint.shape[1], part):
        block = later[low + at : low + at + part]
        joint[0, at : at + part], joint[1, at : at + part] = high_low(product_rows(block, earlier[0], earlier[1]))


def other_kernel(own, own_p, other_p, other, joint):
    other[0], other[1] = high_low(other_p[...])

    def body(chip, core):
        if chip == 1:
            joint_rows(joint, 0, (other_p, own_p)[core], (own, other)[core])

    by_place(body)


def first_kernel(mirror_v, own_v, v0, v1, v2, v3, own, other, own_p, other_p, out_b, out_a, state, joint):
    order = other_p.shape[0]
    rows = out_b.shape[0]
    vectors = (v0[...], v1[...], v2[...], v3[...])
    width = v0.shape[1] - order

    def body(chip, core):
        if chip == 0:
            x = jnp.concatenate([one_row(0, whole_start(vectors, width)), mirror_v[...], own_v[...]], 0)
            for step in range(2):
                maps = (own, other)[step ^ core]
                y = times(stacked(x), maps[0], maps[1])
                x = jnp.concatenate([y[:PAD] + one_row(0, vectors[step ^ core][:, width:]), y[PAD:]], 0)
            state[...] = x[:1]
            out_b[...] = x[PAD : PAD + rows]
            out_a[...] = x[PAD + rows :]
        else:
            joint_rows(joint, joint.shape[1], (other_p, own_p)[core], (own, other)[core])

    by_place(body)


def joint_kernel(v0, v1, own, other, own_p, other_p, joint, joint_f):
    order = own_p.shape[0]
    width = v0.shape[1] - order
    lanes = 128

    def body(chip, core):
        if chip == 0:
            return
        later = (other_p, own_p)[core]
        joint_rows(joint, order - joint.shape[1], later, (own, other)[core])
        first_f, second_f = [(v0, v1)[k ^ core][:, width:] for k in range(2)]
        part = order // PIECES
        for at in range(0, order, part):
            pushed = later[at : at + part] * first_f
            total = pushed[:, :lanes]
            for k in range(lanes, order, lanes):
                total = total + pushed[:, k : k + lanes]
            joint_f[:, at : at + part] = (
                jnp.sum(total.T, axis=0, keepdims=True) + second_f[:, at : at + part]
            )

    by_place(body)


def joint_times(x, parts):
    both = stacked(x)
    return jnp.concatenate([times(both, part[0], part[1]) for part in parts], 1)


def state_rows_kernel(got, state, joint_f, part_0, part_1, part_2, out):
    @pl.when(on_second_chip())
    def _():
        x = jnp.concatenate([one_row(0, state[...]), got[...]], 0)
        y = joint_times(x, (part_0, part_1, part_2))
        out[:PAD] = y[:PAD] + one_row(0, joint_f[...])
        out[PAD:] = y[PAD:]


def rows_kernel(got, part_0, part_1, part_2, out):
    @pl.when(on_second_chip())
    def _():
        out[...] = joint_times(got[...], (part_0, part_1, part_2))


def slice_of(end, place, width):
    mine = end[:, :width]
    for j in range(1, WIN):
        mine = jnp.where(place == j, end[:, j * width : (j + 1) * width], mine)
    return mine


def near_kernel(came, starts, directions, residual, jacobian, end):
    place = lax.axis_index("step") % WIN
    mine = place >= HALF
    end[...] = came[:1]
    jacobian[...] = jnp.where(mine, came[PAD:], 0.0) - directions[...]
    residual[...] = jnp.where(mine, slice_of(came[:1], place, starts.shape[1]), 0.0) - starts[...]


def far_kernel(came, end, residual_in, jacobian_in, residual, jacobian):
    place = lax.axis_index("step") % WIN
    mine = place < HALF
    jacobian[...] = jnp.where(mine, came[...], 0.0) + jacobian_in[...]
    residual[...] = jnp.where(mine, slice_of(end[...], place, residual.shape[1]), 0.0) + residual_in[...]


def call(body, micros, out_shape, *args, specs=None, scratch=(), after=()):
    count, extra = len(args), len(after)

    def run(*refs):
        body(*refs[:count], *refs[count + extra :])

    return pl.pallas_call(
        run,
        out_shape=out_shape,
        in_specs=(specs or [VMEM] * count) + [ANY] * extra,
        out_specs=jax.tree.map(lambda _: VMEM, out_shape),
        scratch_shapes=scratch,
        compiler_params=pltpu.CompilerParams(vmem_limit_bytes=20 << 20),
        cost_estimate=pl.CostEstimate(flops=int(micros * 1e9), bytes_accessed=1, transcendentals=0),
    )(*args, *after)


def local(propagators, forcing, starts, directions):
    own_p, own_v = propagators[0], directions[0]
    order = own_p.shape[0]
    rows = own_v.shape[0]
    steps = lax.axis_size("step")
    block = jax.ShapeDtypeStruct((rows, order), jnp.float32)
    row = jax.ShapeDtypeStruct((1, order), jnp.float32)

    def split(height):
        return jax.ShapeDtypeStruct((2, height, order), jnp.bfloat16)

    other_p = swapped(own_p, 1)
    mirror_v = swapped(own_v, 2)
    vector = jnp.concatenate([starts, forcing], 1)
    vectors = [vector] + [swapped(vector, k) for k in range(1, WIN)]
    own = call(own_kernel, 0.01, split(order), own_p)
    other, part_0 = call(other_kernel, 0.01, [split(order), split(order // 4)], own, own_p, other_p)
    x_b, x_a, state, part_1 = call(
        first_kernel, 3, [block, block, row, split(order // 4)], mirror_v, own_v, *vectors, own, other, own_p, other_p
    )
    got_b, got_a, got_state = swapped(x_b, 2), swapped(x_a, 2), swapped(state, 2)
    part_2, joint_f = call(
        joint_kernel, 1, [split(order // 2), row], *vectors[:2], own, other, own_p, other_p, after=(x_b,)
    )
    joint = part_0, part_1, part_2
    y_b = call(state_rows_kernel, 2, jax.ShapeDtypeStruct((PAD + rows, order), jnp.float32), got_b, got_state, joint_f, *joint)
    to_near = [(i, (i + WIN) % steps if i % WIN >= HALF else i ^ 1) for i in range(steps)]
    to_far = [(i, (i + WIN - HALF) % steps if i % WIN >= HALF else i + HALF) for i in range(steps)]
    near = lax.ppermute(y_b, "step", to_near)
    y_a = call(rows_kernel, 2, block, got_a, *joint, after=(y_b,))
    far = lax.ppermute(y_a, "step", to_far)
    results = [jax.ShapeDtypeStruct(starts.shape, jnp.float32), block]
    *sums, end = call(near_kernel, 1, results + [row], near, starts, own_v)
    residual, jacobian = call(far_kernel, 1, results, far, swapped(end, 2), *sums)
    return residual, jacobian[None]


def solution(mesh):
    return jax.shard_map(
        local,
        mesh=mesh,
        in_specs=(
            P(("parts", "step"), None, None),
            P(("parts", "step"), None),
            P(("parts", "step"), None),
            P(("parts", "step"), None, None),
        ),
        out_specs=(P(("parts", "step"), None), P(("parts", "step"), None, None)),
        check_vma=False,
    )
```

```python
import functools

import jax
import jax.numpy as jnp
from jax import lax
from jax.experimental import pallas as pl
from jax.experimental.pallas import tpu as pltpu
from jax.sharding import PartitionSpec as P

WIN = 4
HALF = WIN // 2
PAD = 8
PIECES = 4
NEAR_PIECES = 2
FAR_PIECES = 2
VMEM = pl.BlockSpec(memory_space=pltpu.VMEM)
ANY = pl.BlockSpec(memory_space=pl.ANY)


def swapped(block, bit):
    count = lax.axis_size("step")
    return lax.ppermute(block, "step", [(i, i ^ bit) for i in range(count)])


def product_nt(left, right):
    return lax.dot_general(left, right, (((1,), (1,)), ((), ())), preferred_element_type=jnp.float32)


def high_low(value):
    high = value.astype(jnp.bfloat16)
    return high, (value - high.astype(jnp.float32)).astype(jnp.bfloat16)


def stacked(x):
    high = x.astype(jnp.bfloat16).astype(jnp.float32)
    return jnp.concatenate([high, x - high], 0).astype(jnp.bfloat16)


def times(both, high, low):
    rows = both.shape[0] // 2
    wide = product_nt(both, high)
    narrow = product_nt(both[: (rows + 15) // 16 * 16], low)
    return wide[:rows] + wide[rows:] + narrow[:rows]


def one_row(at, value):
    row = lax.broadcasted_iota(jnp.int32, (PAD, value.shape[1]), 0)
    return jnp.where(row == at, value, 0.0)


def own_kernel(own_p, maps):
    @pl.when(on_second_chip())
    def _():
        maps[0], maps[1] = high_low(own_p[...])


def whole_start(vectors, width):
    place = lax.axis_index("step") % WIN
    ordered = []
    for j in range(WIN):
        pick = vectors[0][:, :width]
        for flip in range(1, WIN):
            pick = jnp.where(j ^ place == flip, vectors[flip][:, :width], pick)
        ordered.append(pick)
    return jnp.concatenate(ordered, 1)


def on_second_chip():
    return lax.axis_index("step") % WIN >= HALF


def by_place(body):
    place = lax.axis_index("step") % WIN
    for k in range(WIN):
        pl.when(place == k)(functools.partial(body, k // 2, k % 2))


def split_times(x, matrix):
    order = matrix.shape[0]
    part = order // PIECES
    both = stacked(x)
    return jnp.concatenate([times(both, *high_low(matrix[k * part : (k + 1) * part])) for k in range(PIECES)], 1)


def product_rows(later, earlier_high, earlier_low):
    rows = later.shape[0]
    both = stacked(later)
    dot = functools.partial(jnp.dot, preferred_element_type=jnp.float32)
    wide = dot(both, earlier_high)
    return wide[:rows] + wide[rows:] + dot(both[:rows], earlier_low)


def other_kernel(own, own_p, other_p, half, other):
    rows = half.shape[0]
    part = rows // 2

    def body(chip, core):
        if chip == 1:
            other[0], other[1] = high_low(other_p[...])
            earlier, later = (own, other)[core], (other_p, own_p)[core]
            for at in range(0, rows, part):
                block = later[rows * core + at : rows * core + at + part]
                half[at : at + part] = product_rows(block, earlier[0], earlier[1])

    by_place(body)


def first_kernel(mirror_v, own_v, v0, v1, v2, v3, own_p, other_p, state, *outs):
    order = mirror_v.shape[1]
    vectors = (v0[...], v1[...], v2[...], v3[...])
    width = v0.shape[1] - order

    def body(chip, core):
        if chip == 0:
            x = jnp.concatenate([one_row(0, whole_start(vectors, width)), mirror_v[...], own_v[...]], 0)
            for step in range(2):
                y = split_times(x, (own_p, other_p)[step ^ core])
                x = jnp.concatenate([y[:PAD] + one_row(0, vectors[step ^ core][:, width:]), y[PAD:]], 0)
            state[...] = x[:1]
            at = PAD
            for out in outs:
                out[...] = x[at : at + out.shape[0]]
                at += out.shape[0]

    by_place(body)


def joint_kernel(v0, v1, own_p, other_p, own_half, other_half, joint, joint_f):
    order = own_p.shape[0]
    rows = own_half.shape[0]
    width = v0.shape[1] - order
    lanes = 128

    def body(chip, core):
        if chip == 0:
            return
        for k, part in enumerate((own_half, other_half)):
            at = rows * (k ^ core)
            joint[0, at : at + rows], joint[1, at : at + rows] = high_low(part[...])
        later = (other_p, own_p)[core]
        first_f, second_f = [(v0, v1)[k ^ core][:, width:] for k in range(2)]
        part = order // PIECES
        for at in range(0, order, part):
            pushed = later[at : at + part] * first_f
            total = pushed[:, :lanes]
            for k in range(lanes, order, lanes):
                total = total + pushed[:, k : k + lanes]
            joint_f[:, at : at + part] = (
                jnp.sum(total.T, axis=0, keepdims=True) + second_f[:, at : at + part]
            )

    by_place(body)


def state_rows_kernel(got, state, joint, joint_f, out):
    @pl.when(on_second_chip())
    def _():
        x = jnp.concatenate([one_row(0, state[...]), got[...]], 0)
        y = times(stacked(x), joint[0], joint[1])
        out[:PAD] = y[:PAD] + one_row(0, joint_f[...])
        out[PAD:] = y[PAD:]


def rows_kernel(got, joint, out):
    @pl.when(on_second_chip())
    def _():
        out[...] = times(stacked(got[...]), joint[0], joint[1])


def slice_of(end, place, width):
    mine = end[:, :width]
    for j in range(1, WIN):
        mine = jnp.where(place == j, end[:, j * width : (j + 1) * width], mine)
    return mine


def near_kernel(*refs):
    *came, starts, directions, residual, jacobian, end = refs
    place = lax.axis_index("step") % WIN
    mine = place >= HALF
    end[...] = came[0][:1]
    whole = jnp.concatenate([came[0][PAD:]] + [piece[...] for piece in came[1:]], 0)
    jacobian[...] = jnp.where(mine, whole, 0.0) - directions[...]
    residual[...] = jnp.where(mine, slice_of(came[0][:1], place, starts.shape[1]), 0.0) - starts[...]


def far_kernel(*refs):
    *came, end, residual_in, jacobian_in, residual, jacobian = refs
    place = lax.axis_index("step") % WIN
    mine = place < HALF
    whole = jnp.concatenate([piece[...] for piece in came], 0)
    jacobian[...] = jnp.where(mine, whole, 0.0) + jacobian_in[...]
    residual[...] = jnp.where(mine, slice_of(end[...], place, residual.shape[1]), 0.0) + residual_in[...]


def call(body, micros, out_shape, *args, specs=None, scratch=(), after=()):
    count, extra = len(args), len(after)

    def run(*refs):
        body(*refs[:count], *refs[count + extra :])

    return pl.pallas_call(
        run,
        out_shape=out_shape,
        in_specs=(specs or [VMEM] * count) + [ANY] * extra,
        out_specs=jax.tree.map(lambda _: VMEM, out_shape),
        scratch_shapes=scratch,
        compiler_params=pltpu.CompilerParams(vmem_limit_bytes=20 << 20),
        cost_estimate=pl.CostEstimate(flops=int(micros * 1e9), bytes_accessed=1, transcendentals=0),
    )(*args, *after)


def local(propagators, forcing, starts, directions):
    own_p, own_v = propagators[0], directions[0]
    order = own_p.shape[0]
    rows = own_v.shape[0]
    steps = lax.axis_size("step")
    block = jax.ShapeDtypeStruct((rows, order), jnp.float32)
    row = jax.ShapeDtypeStruct((1, order), jnp.float32)

    def split(height):
        return jax.ShapeDtypeStruct((2, height, order), jnp.bfloat16)

    other_p = swapped(own_p, 1)
    mirror_v = swapped(own_v, 2)
    vector = jnp.concatenate([starts, forcing], 1)
    vectors = [vector] + [swapped(vector, k) for k in range(1, WIN)]
    own = call(own_kernel, 0.01, split(order), own_p)
    half_rows = jax.ShapeDtypeStruct((order // 2, order), jnp.float32)
    own_half = call(
        other_kernel, 0.01, half_rows, own, own_p, other_p, scratch=[pltpu.VMEM((2, order, order), jnp.bfloat16)]
    )
    other_half = swapped(own_half, 1)
    heights = [rows // NEAR_PIECES] * NEAR_PIECES + [rows // FAR_PIECES] * FAR_PIECES
    pieces = [jax.ShapeDtypeStruct((height, order), jnp.float32) for height in heights]
    state, *xs = call(first_kernel, 60, [row, *pieces], mirror_v, own_v, *vectors, own_p, other_p)
    got_state = swapped(state, 2)
    got = [swapped(x, 2) for x in xs]
    joint, joint_f = call(
        joint_kernel, 1, [split(order), row], *vectors[:2], own_p, other_p, own_half, other_half, after=(xs[0],)
    )
    to_near = [(i, (i + WIN) % steps if i % WIN >= HALF else i ^ 1) for i in range(steps)]
    to_far = [(i, (i + WIN - HALF) % steps if i % WIN >= HALF else i + HALF) for i in range(steps)]
    done = []
    for k, x in enumerate(got):
        if k == 0:
            tall = jax.ShapeDtypeStruct((PAD + heights[0], order), jnp.float32)
            done.append(call(state_rows_kernel, 2, tall, x, got_state, joint, joint_f))
        else:
            done.append(call(rows_kernel, 2, pieces[k], x, joint, after=done[-1:]))
    near = [lax.ppermute(y, "step", to_near) for y in done[:NEAR_PIECES]]
    far = [lax.ppermute(y, "step", to_far) for y in done[NEAR_PIECES:]]
    results = [jax.ShapeDtypeStruct(starts.shape, jnp.float32), block]
    *sums, end = call(near_kernel, 5, results + [row], *near, starts, own_v)
    residual, jacobian = call(far_kernel, 1, results, *far, swapped(end, 2), *sums)
    return residual, jacobian[None]


def solution(mesh):
    return jax.shard_map(
        local,
        mesh=mesh,
        in_specs=(
            P(("parts", "step"), None, None),
            P(("parts", "step"), None),
            P(("parts", "step"), None),
            P(("parts", "step"), None, None),
        ),
        out_specs=(P(("parts", "step"), None), P(("parts", "step"), None, None)),
        check_vma=False,
    )
```

```python
import functools

import jax
import jax.numpy as jnp
from jax import lax
from jax.experimental import pallas as pl
from jax.experimental.pallas import tpu as pltpu
from jax.sharding import PartitionSpec as P

WIN = 4
HALF = WIN // 2
PAD = 8
PIECES = 4
NEAR_PIECES = 2
FAR_PIECES = 2
VMEM = pl.BlockSpec(memory_space=pltpu.VMEM)
ANY = pl.BlockSpec(memory_space=pl.ANY)


def swapped(block, bit):
    count = lax.axis_size("step")
    return lax.ppermute(block, "step", [(i, i ^ bit) for i in range(count)])


def product_nt(left, right):
    return lax.dot_general(left, right, (((1,), (1,)), ((), ())), preferred_element_type=jnp.float32)


def high_low(value):
    high = value.astype(jnp.bfloat16)
    return high, (value - high.astype(jnp.float32)).astype(jnp.bfloat16)


def stacked(x):
    high = x.astype(jnp.bfloat16).astype(jnp.float32)
    return jnp.concatenate([high, x - high], 0).astype(jnp.bfloat16)


def times(both, high, low):
    rows = both.shape[0] // 2
    wide = product_nt(both, high)
    narrow = product_nt(both[: (rows + 15) // 16 * 16], low)
    return wide[:rows] + wide[rows:] + narrow[:rows]


def one_row(at, value):
    row = lax.broadcasted_iota(jnp.int32, (PAD, value.shape[1]), 0)
    return jnp.where(row == at, value, 0.0)


def own_kernel(own_p, maps):
    @pl.when(on_second_chip())
    def _():
        maps[0], maps[1] = high_low(own_p[...])


def whole_start(vectors, width):
    place = lax.axis_index("step") % WIN
    ordered = []
    for j in range(WIN):
        pick = vectors[0][:, :width]
        for flip in range(1, WIN):
            pick = jnp.where(j ^ place == flip, vectors[flip][:, :width], pick)
        ordered.append(pick)
    return jnp.concatenate(ordered, 1)


def on_second_chip():
    return lax.axis_index("step") % WIN >= HALF


def by_place(body):
    place = lax.axis_index("step") % WIN
    for k in range(WIN):
        pl.when(place == k)(functools.partial(body, k // 2, k % 2))


def split_times(x, matrix):
    order = matrix.shape[0]
    part = order // PIECES
    both = stacked(x)
    return jnp.concatenate([times(both, *high_low(matrix[k * part : (k + 1) * part])) for k in range(PIECES)], 1)


def product_rows(both, earlier_high, earlier_low):
    rows = both.shape[0] // 2
    dot = functools.partial(jnp.dot, preferred_element_type=jnp.float32)
    wide = dot(both, earlier_high)
    return wide[:rows] + wide[rows:] + dot(both[:rows], earlier_low)


def half_kernel(own, own_p, other_p, half):
    rows, order = half.shape
    part = order // PIECES

    def body(chip, core):
        if chip == 1 and core == 0:
            for at in range(0, rows, part):
                half[at : at + part] = product_rows(stacked(other_p[at : at + part]), own[0], own[1])
        elif chip == 1:
            both = stacked(own_p[rows:])
            for at in range(0, order, part):
                here = slice(at, at + part)
                half[:, here] = product_rows(both, *high_low(other_p[:, here]))

    by_place(body)


def first_kernel(mirror_v, own_v, v0, v1, v2, v3, own_p, other_p, state, *outs):
    order = mirror_v.shape[1]
    vectors = (v0[...], v1[...], v2[...], v3[...])
    width = v0.shape[1] - order

    def body(chip, core):
        if chip == 0:
            x = jnp.concatenate([one_row(0, whole_start(vectors, width)), mirror_v[...], own_v[...]], 0)
            for step in range(2):
                y = split_times(x, (own_p, other_p)[step ^ core])
                x = jnp.concatenate([y[:PAD] + one_row(0, vectors[step ^ core][:, width:]), y[PAD:]], 0)
            state[...] = x[:1]
            at = PAD
            for out in outs:
                out[...] = x[at : at + out.shape[0]]
                at += out.shape[0]

    by_place(body)


def joint_kernel(v0, v1, own_p, other_p, own_half, other_half, joint, joint_f):
    order = own_p.shape[0]
    rows = own_half.shape[0]
    width = v0.shape[1] - order
    lanes = 128

    def body(chip, core):
        if chip == 0:
            return
        for k, part in enumerate((own_half, other_half)):
            at = rows * (k ^ core)
            joint[0, at : at + rows], joint[1, at : at + rows] = high_low(part[...])
        later = (other_p, own_p)[core]
        first_f, second_f = [(v0, v1)[k ^ core][:, width:] for k in range(2)]
        part = order // PIECES
        for at in range(0, order, part):
            pushed = later[at : at + part] * first_f
            total = pushed[:, :lanes]
            for k in range(lanes, order, lanes):
                total = total + pushed[:, k : k + lanes]
            joint_f[:, at : at + part] = (
                jnp.sum(total.T, axis=0, keepdims=True) + second_f[:, at : at + part]
            )

    by_place(body)


def state_rows_kernel(got, state, joint, joint_f, out):
    @pl.when(on_second_chip())
    def _():
        x = jnp.concatenate([one_row(0, state[...]), got[...]], 0)
        y = times(stacked(x), joint[0], joint[1])
        out[:PAD] = y[:PAD] + one_row(0, joint_f[...])
        out[PAD:] = y[PAD:]


def rows_kernel(got, joint, out):
    @pl.when(on_second_chip())
    def _():
        out[...] = times(stacked(got[...]), joint[0], joint[1])


def slice_of(end, place, width):
    mine = end[:, :width]
    for j in range(1, WIN):
        mine = jnp.where(place == j, end[:, j * width : (j + 1) * width], mine)
    return mine


def near_kernel(*refs):
    *came, starts, directions, residual, jacobian, end = refs
    place = lax.axis_index("step") % WIN
    mine = place >= HALF
    end[...] = came[0][:1]
    whole = jnp.concatenate([came[0][PAD:]] + [piece[...] for piece in came[1:]], 0)
    jacobian[...] = jnp.where(mine, whole, 0.0) - directions[...]
    residual[...] = jnp.where(mine, slice_of(came[0][:1], place, starts.shape[1]), 0.0) - starts[...]


def far_kernel(*refs):
    *came, end, residual_in, jacobian_in, residual, jacobian = refs
    place = lax.axis_index("step") % WIN
    mine = place < HALF
    whole = jnp.concatenate([piece[...] for piece in came], 0)
    jacobian[...] = jnp.where(mine, whole, 0.0) + jacobian_in[...]
    residual[...] = jnp.where(mine, slice_of(end[...], place, residual.shape[1]), 0.0) + residual_in[...]


def call(body, micros, out_shape, *args, specs=None, scratch=(), after=()):
    count, extra = len(args), len(after)

    def run(*refs):
        body(*refs[:count], *refs[count + extra :])

    return pl.pallas_call(
        run,
        out_shape=out_shape,
        in_specs=(specs or [VMEM] * count) + [ANY] * extra,
        out_specs=jax.tree.map(lambda _: VMEM, out_shape),
        scratch_shapes=scratch,
        compiler_params=pltpu.CompilerParams(vmem_limit_bytes=20 << 20),
        cost_estimate=pl.CostEstimate(flops=int(micros * 1e9), bytes_accessed=1, transcendentals=0),
    )(*args, *after)


def local(propagators, forcing, starts, directions):
    own_p, own_v = propagators[0], directions[0]
    order = own_p.shape[0]
    rows = own_v.shape[0]
    steps = lax.axis_size("step")
    block = jax.ShapeDtypeStruct((rows, order), jnp.float32)
    row = jax.ShapeDtypeStruct((1, order), jnp.float32)

    def split(height):
        return jax.ShapeDtypeStruct((2, height, order), jnp.bfloat16)

    other_p = swapped(own_p, 1)
    mirror_v = swapped(own_v, 2)
    vector = jnp.concatenate([starts, forcing], 1)
    vectors = [vector] + [swapped(vector, k) for k in range(1, WIN)]
    own = call(own_kernel, 0.01, split(order), own_p)
    half_rows = jax.ShapeDtypeStruct((order // 2, order), jnp.float32)
    own_half = call(half_kernel, 0.01, half_rows, own, own_p, other_p)
    other_half = swapped(own_half, 1)
    heights = [rows // NEAR_PIECES] * NEAR_PIECES + [rows // FAR_PIECES] * FAR_PIECES
    pieces = [jax.ShapeDtypeStruct((height, order), jnp.float32) for height in heights]
    state, *xs = call(first_kernel, 60, [row, *pieces], mirror_v, own_v, *vectors, own_p, other_p)
    got_state = swapped(state, 2)
    got = [swapped(x, 2) for x in xs]
    joint, joint_f = call(
        joint_kernel, 1, [split(order), row], *vectors[:2], own_p, other_p, own_half, other_half, after=(xs[0],)
    )
    to_near = [(i, (i + WIN) % steps if i % WIN >= HALF else i ^ 1) for i in range(steps)]
    to_far = [(i, (i + WIN - HALF) % steps if i % WIN >= HALF else i + HALF) for i in range(steps)]
    done = []
    for k, x in enumerate(got):
        if k == 0:
            tall = jax.ShapeDtypeStruct((PAD + heights[0], order), jnp.float32)
            done.append(call(state_rows_kernel, 2, tall, x, got_state, joint, joint_f))
        else:
            done.append(call(rows_kernel, 2, pieces[k], x, joint, after=done[-1:]))
    near = [lax.ppermute(y, "step", to_near) for y in done[:NEAR_PIECES]]
    far = [lax.ppermute(y, "step", to_far) for y in done[NEAR_PIECES:]]
    results = [jax.ShapeDtypeStruct(starts.shape, jnp.float32), block]
    *sums, end = call(near_kernel, 5, results + [row], *near, starts, own_v)
    residual, jacobian = call(far_kernel, 1, results, *far, swapped(end, 2), *sums)
    return residual, jacobian[None]


def solution(mesh):
    return jax.shard_map(
        local,
        mesh=mesh,
        in_specs=(
            P(("parts", "step"), None, None),
            P(("parts", "step"), None),
            P(("parts", "step"), None),
            P(("parts", "step"), None, None),
        ),
        out_specs=(P(("parts", "step"), None), P(("parts", "step"), None, None)),
        check_vma=False,
    )
```

```python
import functools

import jax
import jax.numpy as jnp
from jax import lax
from jax.experimental import pallas as pl
from jax.experimental.pallas import tpu as pltpu
from jax.sharding import PartitionSpec as P

WIN = 4
HALF = WIN // 2
PAD = 8
PIECES = 4
LANES = 128
NEAR_PIECES = 2
FAR_PIECES = 2
VMEM = pl.BlockSpec(memory_space=pltpu.VMEM)
ANY = pl.BlockSpec(memory_space=pl.ANY)


def swapped(block, bit):
    count = lax.axis_size("step")
    return lax.ppermute(block, "step", [(i, i ^ bit) for i in range(count)])


def product_nt(left, right):
    return lax.dot_general(left, right, (((1,), (1,)), ((), ())), preferred_element_type=jnp.float32)


def high_low(value):
    high = value.astype(jnp.bfloat16)
    return high, (value - high.astype(jnp.float32)).astype(jnp.bfloat16)


def stacked(x):
    high = x.astype(jnp.bfloat16).astype(jnp.float32)
    return jnp.concatenate([high, x - high], 0).astype(jnp.bfloat16)


def times(both, high, low):
    rows = both.shape[0] // 2
    wide = product_nt(both, high)
    narrow = product_nt(both[: (rows + 15) // 16 * 16], low)
    return wide[:rows] + wide[rows:] + narrow[:rows]


def put_flat(out, rows, state):
    count = rows.shape[0]
    for k in range(rows.shape[1] // LANES):
        here = slice(k * LANES, (k + 1) * LANES)
        out[k * count : (k + 1) * count] = rows[:, here]
    groups = rows.shape[1] // LANES
    at = groups * count
    out[at : at + groups] = sum(
        jnp.where(
            lax.broadcasted_iota(jnp.int32, (groups, LANES), 0) == k, state[:, k * LANES : (k + 1) * LANES], 0.0
        )
        for k in range(groups)
    )


def take_flat(flat, order):
    groups = order // LANES
    count = flat.shape[0] // groups - 1
    at = groups * count
    rows = jnp.concatenate([flat[k * count : (k + 1) * count] for k in range(groups)], 1)
    state = jnp.concatenate([flat[at + k : at + k + 1] for k in range(groups)], 1)
    return rows, state


def one_row(at, value):
    row = lax.broadcasted_iota(jnp.int32, (PAD, value.shape[1]), 0)
    return jnp.where(row == at, value, 0.0)


def own_kernel(own_p, maps):
    @pl.when(on_second_chip())
    def _():
        maps[0], maps[1] = high_low(own_p[...])


def whole_start(vectors, width):
    place = lax.axis_index("step") % WIN
    ordered = []
    for j in range(WIN):
        pick = vectors[0][:, :width]
        for flip in range(1, WIN):
            pick = jnp.where(j ^ place == flip, vectors[flip][:, :width], pick)
        ordered.append(pick)
    return jnp.concatenate(ordered, 1)


def on_second_chip():
    return lax.axis_index("step") % WIN >= HALF


def by_place(body):
    place = lax.axis_index("step") % WIN
    for k in range(WIN):
        pl.when(place == k)(functools.partial(body, k // 2, k % 2))


def split_times(x, matrix):
    order = matrix.shape[0]
    part = order // PIECES
    both = stacked(x)
    return jnp.concatenate([times(both, *high_low(matrix[k * part : (k + 1) * part])) for k in range(PIECES)], 1)


def product_rows(both, earlier_high, earlier_low):
    rows = both.shape[0] // 2
    dot = functools.partial(jnp.dot, preferred_element_type=jnp.float32)
    wide = dot(both, earlier_high)
    return wide[:rows] + wide[rows:] + dot(both[:rows], earlier_low)


def half_kernel(own, own_p, other_p, half):
    rows, order = half.shape
    part = order // PIECES

    def body(chip, core):
        if chip == 1 and core == 0:
            for at in range(0, rows, part):
                half[at : at + part] = product_rows(stacked(other_p[at : at + part]), own[0], own[1])
        elif chip == 1:
            both = stacked(own_p[rows:])
            for at in range(0, order, part):
                here = slice(at, at + part)
                half[:, here] = product_rows(both, *high_low(other_p[:, here]))

    by_place(body)


def first_kernel(mirror_v, own_v, v0, v1, v2, v3, own_p, other_p, *outs):
    order = mirror_v.shape[1]
    vectors = (v0[...], v1[...], v2[...], v3[...])
    width = v0.shape[1] - order

    def body(chip, core):
        if chip == 0:
            x = jnp.concatenate([one_row(0, whole_start(vectors, width)), mirror_v[...], own_v[...]], 0)
            for step in range(2):
                y = split_times(x, (own_p, other_p)[step ^ core])
                x = jnp.concatenate([y[:PAD] + one_row(0, vectors[step ^ core][:, width:]), y[PAD:]], 0)
            at = PAD + outs[0].shape[0] // (order // LANES) - 1
            put_flat(outs[0], x[PAD:at], x[:1])
            for out in outs[1:]:
                out[...] = x[at : at + out.shape[0]]
                at += out.shape[0]

    by_place(body)


def joint_kernel(v0, v1, own_p, other_p, own_half, other_half, joint, joint_f):
    order = own_p.shape[0]
    rows = own_half.shape[0]
    width = v0.shape[1] - order
    lanes = 128

    def body(chip, core):
        if chip == 0:
            return
        for k, part in enumerate((own_half, other_half)):
            at = rows * (k ^ core)
            joint[0, at : at + rows], joint[1, at : at + rows] = high_low(part[...])
        later = (other_p, own_p)[core]
        first_f, second_f = [(v0, v1)[k ^ core][:, width:] for k in range(2)]
        part = order // PIECES
        for at in range(0, order, part):
            pushed = later[at : at + part] * first_f
            total = pushed[:, :lanes]
            for k in range(lanes, order, lanes):
                total = total + pushed[:, k : k + lanes]
            joint_f[:, at : at + part] = (
                jnp.sum(total.T, axis=0, keepdims=True) + second_f[:, at : at + part]
            )

    by_place(body)


def state_rows_kernel(got, joint, joint_f, out):
    @pl.when(on_second_chip())
    def _():
        rows, state = take_flat(got, joint.shape[2])
        x = jnp.concatenate([one_row(0, state), rows], 0)
        y = times(stacked(x), joint[0], joint[1])
        put_flat(out, y[PAD:], y[:1] + joint_f[...])


def rows_kernel(got, joint, out):
    @pl.when(on_second_chip())
    def _():
        out[...] = times(stacked(got[...]), joint[0], joint[1])


def slice_of(end, place, width):
    mine = end[:, :width]
    for j in range(1, WIN):
        mine = jnp.where(place == j, end[:, j * width : (j + 1) * width], mine)
    return mine


def near_kernel(*refs):
    *came, starts, directions, residual, jacobian, end = refs
    place = lax.axis_index("step") % WIN
    mine = place >= HALF
    rows, came_end = take_flat(came[0], directions.shape[1])
    end[...] = came_end
    whole = jnp.concatenate([rows] + [piece[...] for piece in came[1:]], 0)
    jacobian[...] = jnp.where(mine, whole, 0.0) - directions[...]
    residual[...] = jnp.where(mine, slice_of(came_end, place, starts.shape[1]), 0.0) - starts[...]


def far_kernel(*refs):
    *came, end, residual_in, jacobian_in, residual, jacobian = refs
    place = lax.axis_index("step") % WIN
    mine = place < HALF
    whole = jnp.concatenate([piece[...] for piece in came], 0)
    jacobian[...] = jnp.where(mine, whole, 0.0) + jacobian_in[...]
    residual[...] = jnp.where(mine, slice_of(end[...], place, residual.shape[1]), 0.0) + residual_in[...]


def call(body, micros, out_shape, *args, specs=None, scratch=(), after=()):
    count, extra = len(args), len(after)

    def run(*refs):
        body(*refs[:count], *refs[count + extra :])

    return pl.pallas_call(
        run,
        out_shape=out_shape,
        in_specs=(specs or [VMEM] * count) + [ANY] * extra,
        out_specs=jax.tree.map(lambda _: VMEM, out_shape),
        scratch_shapes=scratch,
        compiler_params=pltpu.CompilerParams(vmem_limit_bytes=20 << 20),
        cost_estimate=pl.CostEstimate(flops=int(micros * 1e9), bytes_accessed=1, transcendentals=0),
    )(*args, *after)


def local(propagators, forcing, starts, directions):
    own_p, own_v = propagators[0], directions[0]
    order = own_p.shape[0]
    rows = own_v.shape[0]
    steps = lax.axis_size("step")
    block = jax.ShapeDtypeStruct((rows, order), jnp.float32)
    row = jax.ShapeDtypeStruct((1, order), jnp.float32)

    def split(height):
        return jax.ShapeDtypeStruct((2, height, order), jnp.bfloat16)

    other_p = swapped(own_p, 1)
    mirror_v = swapped(own_v, 2)
    vector = jnp.concatenate([starts, forcing], 1)
    vectors = [vector] + [swapped(vector, k) for k in range(1, WIN)]
    own = call(own_kernel, 0.01, split(order), own_p)
    half_rows = jax.ShapeDtypeStruct((order // 2, order), jnp.float32)
    own_half = call(half_kernel, 0.01, half_rows, own, own_p, other_p)
    other_half = swapped(own_half, 1)
    heights = [rows // NEAR_PIECES] * NEAR_PIECES + [rows // FAR_PIECES] * FAR_PIECES
    pieces = [jax.ShapeDtypeStruct((height, order), jnp.float32) for height in heights]
    groups = order // LANES
    pieces[0] = jax.ShapeDtypeStruct((groups * (heights[0] + 1), LANES), jnp.float32)
    xs = call(first_kernel, 60, pieces, mirror_v, own_v, *vectors, own_p, other_p)
    got = [swapped(x, 2) for x in xs]
    joint, joint_f = call(
        joint_kernel, 1, [split(order), row], *vectors[:2], own_p, other_p, own_half, other_half, after=(xs[0],)
    )
    to_near = [(i, (i + WIN) % steps if i % WIN >= HALF else i ^ 1) for i in range(steps)]
    to_far = [(i, (i + WIN - HALF) % steps if i % WIN >= HALF else i + HALF) for i in range(steps)]
    done = []
    for k, x in enumerate(got):
        if k == 0:
            done.append(call(state_rows_kernel, 2, pieces[k], x, joint, joint_f))
        else:
            done.append(call(rows_kernel, 2, pieces[k], x, joint, after=done[-1:]))
    near = [lax.ppermute(y, "step", to_near) for y in done[:NEAR_PIECES]]
    far = [lax.ppermute(y, "step", to_far) for y in done[NEAR_PIECES:]]
    results = [jax.ShapeDtypeStruct(starts.shape, jnp.float32), block]
    *sums, end = call(near_kernel, 5, results + [row], *near, starts, own_v)
    residual, jacobian = call(far_kernel, 1, results, *far, swapped(end, 2), *sums)
    return residual, jacobian[None]


def solution(mesh):
    return jax.shard_map(
        local,
        mesh=mesh,
        in_specs=(
            P(("parts", "step"), None, None),
            P(("parts", "step"), None),
            P(("parts", "step"), None),
            P(("parts", "step"), None, None),
        ),
        out_specs=(P(("parts", "step"), None), P(("parts", "step"), None, None)),
        check_vma=False,
    )
```

```python
import functools

import jax
import jax.numpy as jnp
from jax import lax
from jax.experimental import pallas as pl
from jax.experimental.pallas import tpu as pltpu
from jax.sharding import PartitionSpec as P

WIN = 4
HALF = WIN // 2
PAD = 8
PIECES = 4
LANES = 128
VMEM = pl.BlockSpec(memory_space=pltpu.VMEM)
ANY = pl.BlockSpec(memory_space=pl.ANY)


def swapped(block, bit):
    count = lax.axis_size("step")
    return lax.ppermute(block, "step", [(i, i ^ bit) for i in range(count)])


def product_nt(left, right):
    return lax.dot_general(left, right, (((1,), (1,)), ((), ())), preferred_element_type=jnp.float32)


def high_low(value):
    high = value.astype(jnp.bfloat16)
    return high, (value - high.astype(jnp.float32)).astype(jnp.bfloat16)


def stacked(x):
    high = x.astype(jnp.bfloat16).astype(jnp.float32)
    return jnp.concatenate([high, x - high], 0).astype(jnp.bfloat16)


def times(both, high, low):
    rows = both.shape[0] // 2
    wide = product_nt(both, high)
    narrow = product_nt(both[: (rows + 15) // 16 * 16], low)
    return wide[:rows] + wide[rows:] + narrow[:rows]


def put_flat(out, rows, state):
    count = rows.shape[0]
    for k in range(rows.shape[1] // LANES):
        here = slice(k * LANES, (k + 1) * LANES)
        out[k * count : (k + 1) * count] = rows[:, here]
    groups = rows.shape[1] // LANES
    at = groups * count
    out[at : at + groups] = sum(
        jnp.where(
            lax.broadcasted_iota(jnp.int32, (groups, LANES), 0) == k, state[:, k * LANES : (k + 1) * LANES], 0.0
        )
        for k in range(groups)
    )


def take_flat(flat, order):
    groups = order // LANES
    count = flat.shape[0] // groups - 1
    at = groups * count
    rows = jnp.concatenate([flat[k * count : (k + 1) * count] for k in range(groups)], 1)
    state = jnp.concatenate([flat[at + k : at + k + 1] for k in range(groups)], 1)
    return rows, state


def one_row(at, value):
    row = lax.broadcasted_iota(jnp.int32, (PAD, value.shape[1]), 0)
    return jnp.where(row == at, value, 0.0)


def own_kernel(own_p, maps):
    @pl.when(on_second_chip())
    def _():
        maps[0], maps[1] = high_low(own_p[...])


def whole_start(vectors, width):
    place = lax.axis_index("step") % WIN
    ordered = []
    for j in range(WIN):
        pick = vectors[0][:, :width]
        for flip in range(1, WIN):
            pick = jnp.where(j ^ place == flip, vectors[flip][:, :width], pick)
        ordered.append(pick)
    return jnp.concatenate(ordered, 1)


def on_second_chip():
    return lax.axis_index("step") % WIN >= HALF


def by_place(body):
    place = lax.axis_index("step") % WIN
    for k in range(WIN):
        pl.when(place == k)(functools.partial(body, k // 2, k % 2))


def split_times(x, matrix):
    order = matrix.shape[0]
    part = order // PIECES
    both = stacked(x)
    return jnp.concatenate([times(both, *high_low(matrix[k * part : (k + 1) * part])) for k in range(PIECES)], 1)


def product_rows(both, earlier_high, earlier_low):
    rows = both.shape[0] // 2
    dot = functools.partial(jnp.dot, preferred_element_type=jnp.float32)
    wide = dot(both, earlier_high)
    return wide[:rows] + wide[rows:] + dot(both[:rows], earlier_low)


def half_kernel(own, own_p, other_p, half):
    rows, order = half.shape
    part = order // PIECES

    def body(chip, core):
        if chip == 1 and core == 0:
            for at in range(0, rows, part):
                half[at : at + part] = product_rows(stacked(other_p[at : at + part]), own[0], own[1])
        elif chip == 1:
            both = stacked(own_p[rows:])
            for at in range(0, order, part):
                here = slice(at, at + part)
                half[:, here] = product_rows(both, *high_low(other_p[:, here]))

    by_place(body)


def first_kernel(mirror_v, own_v, v0, v1, v2, v3, own_p, other_p, *outs):
    order = mirror_v.shape[1]
    vectors = (v0[...], v1[...], v2[...], v3[...])
    width = v0.shape[1] - order

    def body(chip, core):
        if chip == 0:
            half = mirror_v.shape[0] // 2
            x = [one_row(0, whole_start(vectors, width)), mirror_v[:half], own_v[...], mirror_v[half:]]
            x = jnp.concatenate(x, 0)
            for step in range(2):
                y = split_times(x, (own_p, other_p)[step ^ core])
                x = jnp.concatenate([y[:PAD] + one_row(0, vectors[step ^ core][:, width:]), y[PAD:]], 0)
            at = PAD + outs[0].shape[0] // (order // LANES) - 1
            put_flat(outs[0], x[PAD:at], x[:1])
            for out in outs[1:]:
                out[...] = x[at : at + out.shape[0]]
                at += out.shape[0]

    by_place(body)


def joint_kernel(v0, v1, own_p, other_p, own_half, other_half, joint, joint_f):
    order = own_p.shape[0]
    rows = own_half.shape[0]
    width = v0.shape[1] - order
    lanes = 128

    def body(chip, core):
        if chip == 0:
            return
        for k, part in enumerate((own_half, other_half)):
            at = rows * (k ^ core)
            joint[0, at : at + rows], joint[1, at : at + rows] = high_low(part[...])
        later = (other_p, own_p)[core]
        first_f, second_f = [(v0, v1)[k ^ core][:, width:] for k in range(2)]
        part = order // PIECES
        for at in range(0, order, part):
            pushed = later[at : at + part] * first_f
            total = pushed[:, :lanes]
            for k in range(lanes, order, lanes):
                total = total + pushed[:, k : k + lanes]
            joint_f[:, at : at + part] = (
                jnp.sum(total.T, axis=0, keepdims=True) + second_f[:, at : at + part]
            )

    by_place(body)


def state_rows_kernel(got, joint, joint_f, out):
    @pl.when(on_second_chip())
    def _():
        rows, state = take_flat(got, joint.shape[2])
        x = jnp.concatenate([one_row(0, state), rows], 0)
        y = times(stacked(x), joint[0], joint[1])
        put_flat(out, y[PAD:], y[:1] + joint_f[...])


def rows_kernel(got, joint, out):
    @pl.when(on_second_chip())
    def _():
        out[...] = times(stacked(got[...]), joint[0], joint[1])


def slice_of(end, place, width):
    mine = end[:, :width]
    for j in range(1, WIN):
        mine = jnp.where(place == j, end[:, j * width : (j + 1) * width], mine)
    return mine


def end_kernel(came, end):
    groups = end.shape[1] // LANES
    at = came.shape[0] - groups
    end[...] = jnp.concatenate([came[at + k : at + k + 1] for k in range(groups)], 1)


def middle_kernel(near, far_0, far_1, starts, directions, residual, jacobian):
    place = lax.axis_index("step") % WIN
    first = place < HALF
    rows, end = take_flat(near, directions.shape[1])
    count = rows.shape[0]
    jacobian[:count] = jnp.where(first, far_0[...], rows) - directions[:count]
    jacobian[count:] = jnp.where(first, far_1[...], 0.0) - directions[count:]
    residual[...] = jnp.where(first, 0.0, slice_of(end, place, starts.shape[1])) - starts[...]


def last_kernel(near, mirror_end, residual_in, jacobian_in, residual, jacobian):
    place = lax.axis_index("step") % WIN
    first = place < HALF
    count = jacobian.shape[0] - near.shape[0]
    jacobian[:count] = jacobian_in[:count]
    jacobian[count:] = jnp.where(first, 0.0, near[...]) + jacobian_in[count:]
    here = slice_of(mirror_end[...], place, residual.shape[1])
    residual[...] = jnp.where(first, here, 0.0) + residual_in[...]


def call(body, micros, out_shape, *args, specs=None, scratch=(), after=()):
    count, extra = len(args), len(after)

    def run(*refs):
        body(*refs[:count], *refs[count + extra :])

    return pl.pallas_call(
        run,
        out_shape=out_shape,
        in_specs=(specs or [VMEM] * count) + [ANY] * extra,
        out_specs=jax.tree.map(lambda _: VMEM, out_shape),
        scratch_shapes=scratch,
        compiler_params=pltpu.CompilerParams(vmem_limit_bytes=20 << 20),
        cost_estimate=pl.CostEstimate(flops=int(micros * 1e9), bytes_accessed=1, transcendentals=0),
    )(*args, *after)


def local(propagators, forcing, starts, directions):
    own_p, own_v = propagators[0], directions[0]
    order = own_p.shape[0]
    rows = own_v.shape[0]
    steps = lax.axis_size("step")
    block = jax.ShapeDtypeStruct((rows, order), jnp.float32)
    row = jax.ShapeDtypeStruct((1, order), jnp.float32)

    def split(height):
        return jax.ShapeDtypeStruct((2, height, order), jnp.bfloat16)

    other_p = swapped(own_p, 1)
    mirror_v = swapped(own_v, 2)
    vector = jnp.concatenate([starts, forcing], 1)
    vectors = [vector] + [swapped(vector, k) for k in range(1, WIN)]
    own = call(own_kernel, 0.01, split(order), own_p)
    half_rows = jax.ShapeDtypeStruct((order // 2, order), jnp.float32)
    own_half = call(half_kernel, 0.01, half_rows, own, own_p, other_p)
    other_half = swapped(own_half, 1)
    heights = [rows // 2] * 4
    pieces = [jax.ShapeDtypeStruct((height, order), jnp.float32) for height in heights]
    groups = order // LANES
    pieces[0] = jax.ShapeDtypeStruct((groups * (heights[0] + 1), LANES), jnp.float32)
    xs = call(first_kernel, 60, pieces, mirror_v, own_v, *vectors, own_p, other_p)
    got = [swapped(x, 2) for x in xs]
    joint, joint_f = call(
        joint_kernel, 1, [split(order), row], *vectors[:2], own_p, other_p, own_half, other_half, after=(xs[0],)
    )
    to_near = [(i, (i + WIN) % steps if i % WIN >= HALF else i ^ 1) for i in range(steps)]
    to_far = [(i, (i + WIN - HALF) % steps) for i in range(steps) if i % WIN >= HALF]
    done = []
    for k, x in enumerate(got):
        if k == 0:
            done.append(call(state_rows_kernel, 2, pieces[k], x, joint, joint_f))
        else:
            done.append(call(rows_kernel, 2, pieces[k], x, joint, after=done[-1:]))
    routes = to_near, to_far, to_far, to_near
    near_0, far_0, far_1, near_1 = (lax.ppermute(y, "step", route) for y, route in zip(done, routes))
    end = call(end_kernel, 0.01, row, near_0)
    results = [jax.ShapeDtypeStruct(starts.shape, jnp.float32), block]
    sums = call(middle_kernel, 5, results, near_0, far_0, far_1, starts, own_v)
    residual, jacobian = call(last_kernel, 1, results, near_1, swapped(end, 2), *sums)
    return residual, jacobian[None]


def solution(mesh):
    return jax.shard_map(
        local,
        mesh=mesh,
        in_specs=(
            P(("parts", "step"), None, None),
            P(("parts", "step"), None),
            P(("parts", "step"), None),
            P(("parts", "step"), None, None),
        ),
        out_specs=(P(("parts", "step"), None), P(("parts", "step"), None, None)),
        check_vma=False,
    )
```

```python
import functools

import jax
import jax.numpy as jnp
from jax import lax
from jax.experimental import pallas as pl
from jax.experimental.pallas import tpu as pltpu
from jax.sharding import PartitionSpec as P

WIN = 4
HALF = WIN // 2
PAD = 8
PIECES = 4
LANES = 128
VMEM = pl.BlockSpec(memory_space=pltpu.VMEM)
ANY = pl.BlockSpec(memory_space=pl.ANY)


def swapped(block, bit):
    count = lax.axis_size("step")
    return lax.ppermute(block, "step", [(i, i ^ bit) for i in range(count)])


def product_nt(left, right):
    return lax.dot_general(left, right, (((1,), (1,)), ((), ())), preferred_element_type=jnp.float32)


def high_low(value):
    high = value.astype(jnp.bfloat16)
    return high, (value - high.astype(jnp.float32)).astype(jnp.bfloat16)


def stacked(x):
    high = x.astype(jnp.bfloat16).astype(jnp.float32)
    return jnp.concatenate([high, x - high], 0).astype(jnp.bfloat16)


def times(both, high, low):
    rows = both.shape[0] // 2
    wide = product_nt(both, high)
    narrow = product_nt(both[: (rows + 15) // 16 * 16], low)
    return wide[:rows] + wide[rows:] + narrow[:rows]


def put_flat(out, rows, state):
    count = rows.shape[0]
    for k in range(rows.shape[1] // LANES):
        here = slice(k * LANES, (k + 1) * LANES)
        out[k * count : (k + 1) * count] = rows[:, here]
    groups = rows.shape[1] // LANES
    at = groups * count
    out[at : at + groups] = sum(
        jnp.where(
            lax.broadcasted_iota(jnp.int32, (groups, LANES), 0) == k, state[:, k * LANES : (k + 1) * LANES], 0.0
        )
        for k in range(groups)
    )


def take_flat(flat, order):
    groups = order // LANES
    count = flat.shape[0] // groups - 1
    at = groups * count
    rows = jnp.concatenate([flat[k * count : (k + 1) * count] for k in range(groups)], 1)
    state = jnp.concatenate([flat[at + k : at + k + 1] for k in range(groups)], 1)
    return rows, state


def one_row(at, value):
    row = lax.broadcasted_iota(jnp.int32, (PAD, value.shape[1]), 0)
    return jnp.where(row == at, value, 0.0)


def own_kernel(own_p, maps):
    @pl.when(on_second_chip())
    def _():
        maps[0], maps[1] = high_low(own_p[...])


def whole_start(vectors, width):
    place = lax.axis_index("step") % WIN
    ordered = []
    for j in range(WIN):
        pick = vectors[0][:, :width]
        for flip in range(1, WIN):
            pick = jnp.where(j ^ place == flip, vectors[flip][:, :width], pick)
        ordered.append(pick)
    return jnp.concatenate(ordered, 1)


def on_second_chip():
    return lax.axis_index("step") % WIN >= HALF


def by_place(body):
    place = lax.axis_index("step") % WIN
    for k in range(WIN):
        pl.when(place == k)(functools.partial(body, k // 2, k % 2))


def split_times(x, matrix):
    order = matrix.shape[0]
    part = order // PIECES
    both = stacked(x)
    return jnp.concatenate([times(both, *high_low(matrix[k * part : (k + 1) * part])) for k in range(PIECES)], 1)


def product_rows(both, earlier_high, earlier_low):
    rows = both.shape[0] // 2
    dot = functools.partial(jnp.dot, preferred_element_type=jnp.float32)
    wide = dot(both, earlier_high)
    return wide[:rows] + wide[rows:] + dot(both[:rows], earlier_low)


def half_kernel(own, own_p, other_p, half):
    rows, order = half.shape
    part = order // PIECES

    def body(chip, core):
        if chip == 1 and core == 0:
            for at in range(0, rows, part):
                half[at : at + part] = product_rows(stacked(other_p[at : at + part]), own[0], own[1])
        elif chip == 1:
            both = stacked(own_p[rows:])
            for at in range(0, order, part):
                here = slice(at, at + part)
                half[:, here] = product_rows(both, *high_low(other_p[:, here]))

    by_place(body)


def first_kernel(mirror_v, own_v, v0, v1, v2, v3, own_p, other_p, *outs):
    order = mirror_v.shape[1]
    vectors = (v0[...], v1[...], v2[...], v3[...])
    width = v0.shape[1] - order

    def body(chip, core):
        if chip == 0:
            half = mirror_v.shape[0] // 2
            x = [one_row(0, whole_start(vectors, width)), mirror_v[:half], own_v[...], mirror_v[half:]]
            x = jnp.concatenate(x, 0)
            for step in range(2):
                y = split_times(x, (own_p, other_p)[step ^ core])
                x = jnp.concatenate([y[:PAD] + one_row(0, vectors[step ^ core][:, width:]), y[PAD:]], 0)
            at = PAD + outs[0].shape[0] // (order // LANES) - 1
            put_flat(outs[0], x[PAD:at], x[:1])
            for out in outs[1:]:
                out[...] = x[at : at + out.shape[0]]
                at += out.shape[0]

    by_place(body)


def joint_kernel(v0, v1, own_p, other_p, own_half, other_half, joint, joint_f):
    order = own_p.shape[0]
    rows = own_half.shape[0]
    width = v0.shape[1] - order
    lanes = 128

    def body(chip, core):
        if chip == 0:
            return
        for k, part in enumerate((own_half, other_half)):
            at = rows * (k ^ core)
            joint[0, at : at + rows], joint[1, at : at + rows] = high_low(part[...])
        later = (other_p, own_p)[core]
        first_f, second_f = [(v0, v1)[k ^ core][:, width:] for k in range(2)]
        part = order // PIECES
        for at in range(0, order, part):
            pushed = later[at : at + part] * first_f
            total = pushed[:, :lanes]
            for k in range(lanes, order, lanes):
                total = total + pushed[:, k : k + lanes]
            joint_f[:, at : at + part] = (
                jnp.sum(total.T, axis=0, keepdims=True) + second_f[:, at : at + part]
            )

    by_place(body)


def state_rows_kernel(got, joint, joint_f, out):
    @pl.when(on_second_chip())
    def _():
        rows, state = take_flat(got, joint.shape[2])
        x = jnp.concatenate([one_row(0, state), rows], 0)
        y = times(stacked(x), joint[0], joint[1])
        put_flat(out, y[PAD:], y[:1] + joint_f[...])


def rows_kernel(got, joint, out):
    @pl.when(on_second_chip())
    def _():
        out[...] = times(stacked(got[...]), joint[0], joint[1])


def slice_of(end, place, width):
    mine = end[:, :width]
    for j in range(1, WIN):
        mine = jnp.where(place == j, end[:, j * width : (j + 1) * width], mine)
    return mine


def end_kernel(came, end):
    groups = end.shape[1] // LANES
    at = came.shape[0] - groups
    end[...] = jnp.concatenate([came[at + k : at + k + 1] for k in range(groups)], 1)


def middle_kernel(near, far_0, far_1, starts, directions, residual, jacobian):
    place = lax.axis_index("step") % WIN
    first = place < HALF
    rows, end = take_flat(near, directions.shape[1])
    count = rows.shape[0]
    jacobian[:count] = jnp.where(first, far_0[...], rows) - directions[:count]
    jacobian[count:] = jnp.where(first, far_1[...], 0.0) - directions[count:]
    residual[...] = jnp.where(first, 0.0, slice_of(end, place, starts.shape[1])) - starts[...]


def last_kernel(near, mirror_end, residual_in, jacobian_in, residual, jacobian):
    place = lax.axis_index("step") % WIN
    first = place < HALF
    count = jacobian.shape[0] - near.shape[0]
    jacobian[:count] = jacobian_in[:count]
    jacobian[count:] = jnp.where(first, 0.0, near[...]) + jacobian_in[count:]
    here = slice_of(mirror_end[...], place, residual.shape[1])
    residual[...] = jnp.where(first, here, 0.0) + residual_in[...]


def call(body, micros, out_shape, *args, specs=None, scratch=(), after=()):
    count, extra = len(args), len(after)

    def run(*refs):
        body(*refs[:count], *refs[count + extra :])

    return pl.pallas_call(
        run,
        out_shape=out_shape,
        in_specs=(specs or [VMEM] * count) + [ANY] * extra,
        out_specs=jax.tree.map(lambda _: VMEM, out_shape),
        scratch_shapes=scratch,
        compiler_params=pltpu.CompilerParams(vmem_limit_bytes=20 << 20),
        cost_estimate=pl.CostEstimate(flops=int(micros * 1e9), bytes_accessed=1, transcendentals=0),
    )(*args, *after)


def local(propagators, forcing, starts, directions):
    own_p, own_v = propagators[0], directions[0]
    order = own_p.shape[0]
    rows = own_v.shape[0]
    steps = lax.axis_size("step")
    block = jax.ShapeDtypeStruct((rows, order), jnp.float32)
    row = jax.ShapeDtypeStruct((1, order), jnp.float32)

    def split(height):
        return jax.ShapeDtypeStruct((2, height, order), jnp.bfloat16)

    other_p = swapped(own_p, 1)
    mirror_v = swapped(own_v, 2)
    vector = jnp.concatenate([starts, forcing], 1)
    vectors = [vector] + [swapped(vector, k) for k in range(1, WIN)]
    own = call(own_kernel, 0.01, split(order), own_p)
    half_rows = jax.ShapeDtypeStruct((order // 2, order), jnp.float32)
    own_half = call(half_kernel, 0.01, half_rows, own, own_p, other_p)
    other_half = swapped(own_half, 1)
    heights = [rows // 2] * 4
    pieces = [jax.ShapeDtypeStruct((height, order), jnp.float32) for height in heights]
    groups = order // LANES
    pieces[0] = jax.ShapeDtypeStruct((groups * (heights[0] + 1), LANES), jnp.float32)
    xs = call(first_kernel, 60, pieces, mirror_v, own_v, *vectors, own_p, other_p)
    to_second = [(i, i + HALF) for i in range(steps) if i % WIN < HALF]
    got = [swapped(x, 2) for x in xs[:3]] + [lax.ppermute(x, "step", to_second) for x in xs[3:]]
    joint, joint_f = call(
        joint_kernel, 1, [split(order), row], *vectors[:2], own_p, other_p, own_half, other_half, after=(xs[0],)
    )
    to_near = [(i, (i + WIN) % steps if i % WIN >= HALF else i ^ 1) for i in range(steps)]
    to_far = [(i, (i + WIN - HALF) % steps) for i in range(steps) if i % WIN >= HALF]
    done = []
    for k, x in enumerate(got):
        if k == 0:
            done.append(call(state_rows_kernel, 2, pieces[k], x, joint, joint_f))
        else:
            done.append(call(rows_kernel, 2, pieces[k], x, joint, after=done[-1:]))
    routes = to_near, to_far, to_far, to_near
    near_0, far_0, far_1, near_1 = (lax.ppermute(y, "step", route) for y, route in zip(done, routes))
    end = call(end_kernel, 0.01, row, near_0)
    results = [jax.ShapeDtypeStruct(starts.shape, jnp.float32), block]
    sums = call(middle_kernel, 5, results, near_0, far_0, far_1, starts, own_v)
    residual, jacobian = call(last_kernel, 1, results, near_1, swapped(end, 2), *sums)
    return residual, jacobian[None]


def solution(mesh):
    return jax.shard_map(
        local,
        mesh=mesh,
        in_specs=(
            P(("parts", "step"), None, None),
            P(("parts", "step"), None),
            P(("parts", "step"), None),
            P(("parts", "step"), None, None),
        ),
        out_specs=(P(("parts", "step"), None), P(("parts", "step"), None, None)),
        check_vma=False,
    )
```
